256 devices in a mesh: branch: 4 (over y), seq: 16 (over z_lo, x, core), mp: 4 (over z_hi).
Axes of the slice: x: 4, y: 4, z: 8 (z_hi: 4, z_lo: 2; z = z_hi * 2 + z_lo), core: 2. Of those that a mesh axis runs over, the one named last changes fastest.
Arguments:
- span_q: bfloat16 [4, 2048, 2560], P('branch', 'seq', 'mp'), may hold values from -6 to 6
- span_k: bfloat16 [4, 2048, 2560], P('branch', 'seq', 'mp'), may hold values from -6 to 6
- span_v: bfloat16 [4, 2048, 2560], P('branch', 'seq', 'mp'), may hold values from -6 to 6
- hist_k: bfloat16 [4, 8192, 2560], P('branch', 'seq', 'mp'), may hold values from -6 to 6
- hist_v: bfloat16 [4, 8192, 2560], P('branch', 'seq', 'mp'), may hold values from -6 to 6
- hist_len: int32 [4], replicated, may hold values from 0 to 8192, as said below
- group_branch: int32 [4], replicated, may hold values from 0 to 3, each once
- guidance_w: float32 [4], replicated, may hold values from -1 to 2
- frame_level: int32 [32], replicated, may hold values from 0 to 31
- residual: bfloat16 [4, 2048, 5120], P('branch', ('seq', 'mp')), may hold values from -0.59765625 to 0.59765625
- out_weight: bfloat16 [2560, 5120], P('mp'), may hold values from -0.75 to 0.75
- mod_table: float32 [32, 2, 5120], replicated, may hold values from -3 to 3
- head_weight: bfloat16 [5120, 64], replicated, may hold values from -0.078125 to 0.078125
Outputs:
- velocity: float32 [2048, 64], P(('seq', 'mp'))
The draws below stay inside these ranges and needn't reach their ends.
Inputs may be any that keep to these rules, and one draw needn't show every extreme that they name: `hist_len`: one branch attends to all 8192 history tokens and one to none.
All inputs are finite; a program needn't handle non-finite values.
Results may differ from the reference program's by a relative error of at most 0.017.
Values may be sent and summed in bfloat16 or wider, within the bound.
No kernel may reach another device: no remote copies, remote signals or barrier semaphores. Data moves between devices by JAX's collectives and lax.ppermute only.
A program may use at most 128 MiB of HBM per device.

```python
import jax
import jax.numpy as jnp
from jax import lax

D = 5120
HEADS = 20
HSZ = 128
OUTC = 64
FRAME_TOK = 64
LEVELS = 32
BR = 4
SPAN = 2048
HIST = 8192
HD = 2560
FRAMES = 32


def draw_span_q(key, part):
    key = jax.random.fold_in(key, 11)
    base = jnp.clip(jax.random.normal(key, (BR, SPAN, HD), jnp.float32), -5.0, 5.0)
    return base.astype(jnp.bfloat16)


def draw_span_k(key, part):
    key = jax.random.fold_in(key, 12)
    base = jnp.clip(jax.random.normal(key, (BR, SPAN, HD), jnp.float32), -5.0, 5.0)
    return base.astype(jnp.bfloat16)


def draw_hist_len(key, part):
    key = jax.random.fold_in(key, 5)
    first, second = jax.random.split(key)
    middle = jax.random.randint(first, (2,), 1, HIST)
    values = jnp.concatenate([jnp.array([HIST, 0], jnp.int32), middle.astype(jnp.int32)])
    order = jax.random.permutation(second, 4)
    return values[order]


def touch_ends(result, own_key, smallest, high):
    extent = result.shape
    spot = [jax.random.randint(jax.random.fold_in(own_key, axis), (), 0, extent[axis]) for axis in range(len(extent))]
    result = result.at[tuple(spot)].set(smallest)
    longest = extent.index(max(extent))
    spot[longest] = (spot[longest] + 1) % extent[longest]
    return result.at[tuple(spot)].set(high)


def shard_levels(own_key, extent, cuts, smallest, top_value):
    loudness = 1.0
    for dim, blocks in cuts:
        steps = jax.random.uniform(jax.random.fold_in(jax.random.fold_in(own_key, 6), dim), (blocks,), jnp.float32, smallest / len(cuts), top_value / len(cuts))
        loudness = loudness * jnp.repeat(jnp.exp(steps), extent[dim] // blocks).reshape((-1,) + (1,) * (len(extent) - 1 - dim))
    return loudness


def bell_draw(rng, extent, spread, bound, pieces=(), held_as=jnp.bfloat16):
    result = jax.random.normal(rng, extent, jnp.float32) * spread
    if len(pieces) > 0:
        result = shard_levels(rng, extent, pieces, -0.22, 0.18) * result
    return jnp.clip(result, min=-bound, max=bound).astype(held_as)


def setup_inputs(seed: int = 0) -> dict:
    key_list = jax.random.split(jax.random.key(seed), 14)
    return {
        "span_q": draw_span_q(jax.random.fold_in(key_list[13], 71), 0),
        "span_k": draw_span_k(jax.random.fold_in(key_list[13], 71), 0),
        "span_v": bell_draw(key_list[2], (BR, SPAN, HD), 1.0, 6.0, ((0, 4), (1, 16), (2, 4))),
        "hist_k": bell_draw(key_list[3], (BR, HIST, HD), 1.0, 6.0, ((0, 4), (1, 16), (2, 4))),
        "hist_v": bell_draw(key_list[4], (BR, HIST, HD), 1.0, 6.0, ((0, 4), (1, 16), (2, 4))),
        "hist_len": draw_hist_len(jax.random.fold_in(key_list[13], 71), 0),
        "group_branch": jax.random.permutation(key_list[6], BR).astype(jnp.int32),
        "guidance_w": jnp.clip(jax.random.uniform(key_list[7], (BR,), jnp.float32, -1.0, 2.0), -1.0, 2.0),
        "frame_level": touch_ends(jax.random.randint(key_list[8], (FRAMES,), 0, LEVELS), jax.random.fold_in(key_list[8], 1), 0, LEVELS - 1).astype(jnp.int32),
        "residual": bell_draw(key_list[9], (BR, SPAN, D), 0.1, 0.59765625, ((0, 4), (1, 64))),
        "out_weight": bell_draw(key_list[10], (HD, D), 64 ** -0.5, 0.75, ((0, 4),)),
        "mod_table": bell_draw(key_list[11], (LEVELS, 2, D), 0.5, 3.0, (), jnp.float32),
        "head_weight": bell_draw(key_list[12], (D, OUTC), D ** -0.5, 0.078125),
    }


NEG = -1e+30

def attend_head(inputs, valid):
    queries, keys, values = inputs
    scores = jnp.dot(queries, keys.T, preferred_element_type=jnp.float32) * HSZ ** (-0.5)
    scores = jnp.where(valid[None, :], scores, NEG)
    peak = lax.optimization_barrier(jnp.max(scores, axis=1, keepdims=True))
    weights = jnp.where(valid[None, :], jnp.exp(scores - peak), 0.0)
    total = lax.optimization_barrier(jnp.sum(weights, axis=1, keepdims=True))
    summed = jnp.dot(weights.astype(jnp.bfloat16), values, preferred_element_type=jnp.float32)
    return summed / total

def reference(span_q, span_k, span_v, hist_k, hist_v, hist_len, group_branch, guidance_w, frame_level, residual, out_weight, mod_table, head_weight):
    positions = jnp.arange(SPAN)
    levels = frame_level[positions // FRAME_TOK]
    shift = mod_table[levels, 0]
    scale = mod_table[levels, 1]
    velocity = jnp.zeros((SPAN, OUTC), jnp.float32)
    for group in range(BR):
        branch_id = group_branch[group]
        length = hist_len[branch_id]
        valid = jnp.concatenate([jnp.ones((SPAN,), bool), jnp.arange(HIST) < length])
        keys = jnp.concatenate([span_k[group], hist_k[group]], axis=0)
        values = jnp.concatenate([span_v[group], hist_v[group]], axis=0)
        per_q = span_q[group].reshape(SPAN, HEADS, HSZ).transpose(1, 0, 2)
        per_k = keys.reshape(-1, HEADS, HSZ).transpose(1, 0, 2)
        per_v = values.reshape(-1, HEADS, HSZ).transpose(1, 0, 2)
        heads_out = lax.map(lambda item: attend_head(item, valid), (per_q, per_k, per_v))
        attended = heads_out.transpose(1, 0, 2).reshape(SPAN, HD).astype(jnp.bfloat16)
        stream = residual[group].astype(jnp.float32) + jnp.dot(attended, out_weight, preferred_element_type=jnp.float32)
        mean = lax.optimization_barrier(jnp.mean(stream, axis=1, keepdims=True))
        centred = stream - mean
        variance = lax.optimization_barrier(jnp.mean(centred * centred, axis=1, keepdims=True))
        normed = centred * lax.rsqrt(variance + 1e-06)
        modulated = (normed * (1.0 + scale) + shift).astype(jnp.bfloat16)
        branch_velocity = jnp.dot(modulated, head_weight, preferred_element_type=jnp.float32)
        velocity = velocity + guidance_w[branch_id] * branch_velocity
    return velocity
```

```python
import functools

import jax
import jax.numpy as jnp
from jax import lax
from jax.experimental import pallas as pl
from jax.experimental.pallas import tpu as pltpu
from jax.sharding import PartitionSpec as P

HSZ = 128
FRAME_TOK = 64
NEG = -1e30
STAT_ROWS = 16
SCORE_TO_EXP2 = HSZ ** (-0.5) * 1.4426950408889634

XS = 4


def hop(dz, dx, dc):
    return [
        ((z * XS + x) * 2 + c, ((z ^ dz) * XS + (x + dx) % XS) * 2 + (c ^ dc))
        for z in range(2)
        for x in range(XS)
        for c in range(2)
    ]


def turn(step, count=4):
    return [(i, (i + step) % count) for i in range(count)]


def attend_kernel(blocks, width, hist_len, group_branch, *refs):
    queries = refs[:blocks]
    keys = refs[blocks : blocks + 4]
    values = refs[blocks + 4 : blocks + 8]
    sent = refs[blocks + 8 : 2 * blocks + 8]
    turned = refs[2 * blocks + 8]
    rows, feat = queries[0].shape
    heads = feat // HSZ
    sizes = [k.shape[0] for k in keys]
    length = hist_len[group_branch[lax.axis_index("branch")]]
    seq = lax.axis_index("seq")
    other = seq + 1 - 2 * lax.rem(seq, 2)
    for h in range(heads):
        cols = slice(h * HSZ, (h + 1) * HSZ)
        at = 0
        for value, size in zip(values, sizes):
            turned[cols, at : at + size] = value[:, cols].T
            at += size
    for first in range(0, blocks, width):
        stats = []
        for h in range(heads):
            cols = slice(h * HSZ, (h + 1) * HSZ)
            q = jnp.concatenate([queries[first + i][:, cols] for i in range(width)], axis=0)
            scores = []
            for j, key in enumerate(keys):
                s = lax.dot_general(
                    key[:, cols], q, (((1,), (1,)), ((), ())), preferred_element_type=jnp.float32
                )
                if j >= 2:
                    start = (seq if j == 2 else other) * sizes[j]
                    spot = start + lax.broadcasted_iota(jnp.int32, s.shape, 0)
                    s = jnp.where(spot < length, s, NEG)
                scores.append(s)
            peak = functools.reduce(
                jnp.maximum, [jnp.max(s, axis=0, keepdims=True) for s in scores]
            )
            total, summed, at = 0.0, 0.0, 0
            for s, size in zip(scores, sizes):
                weight = jnp.exp2((s - peak) * SCORE_TO_EXP2)
                total = total + jnp.sum(weight, axis=0, keepdims=True)
                summed = summed + jnp.dot(
                    turned[cols, at : at + size],
                    weight.astype(jnp.bfloat16),
                    preferred_element_type=jnp.float32,
                )
                at += size
            out = (summed / total).astype(jnp.bfloat16)
            for i in range(width):
                sent[first + i][cols, :] = out[:, i * rows : (i + 1) * rows]
            level = peak * SCORE_TO_EXP2 + jnp.log2(total)
            high = level.astype(jnp.bfloat16).astype(jnp.float32)
            middle = (level - high).astype(jnp.bfloat16).astype(jnp.float32)
            stats += [high, middle, level - high - middle]
        stats.append(jnp.zeros((STAT_ROWS - len(stats), stats[0].shape[1]), jnp.float32))
        stats = jnp.concatenate(stats, axis=0).astype(jnp.bfloat16)
        for i in range(width):
            sent[first + i][feat:, :] = stats[:, i * rows : (i + 1) * rows]


def attend(hist_len, group_branch, queries, keys, values, width):
    blocks = len(queries)
    rows, feat = queries[0].shape
    count = sum(k.shape[0] for k in keys)
    vmem = pl.BlockSpec(memory_space=pltpu.VMEM)
    smem = pl.BlockSpec(memory_space=pltpu.SMEM)
    return pl.pallas_call(
        functools.partial(attend_kernel, blocks, width),
        out_shape=[jax.ShapeDtypeStruct((feat + STAT_ROWS, rows), jnp.bfloat16)] * blocks,
        in_specs=[smem, smem] + [vmem] * (blocks + 8),
        out_specs=[vmem] * blocks,
        scratch_shapes=[pltpu.VMEM((feat, count), jnp.bfloat16)],
        compiler_params=pltpu.CompilerParams(vmem_limit_bytes=40 * 2**20),
        cost_estimate=pl.CostEstimate(
            flops=4 * blocks * rows * count * feat,
            bytes_accessed=4 * count * feat,
            transcendentals=blocks * rows * count * (feat // HSZ),
        ),
        name="attend",
    )(hist_len, group_branch, *queries, *keys, *values)


def project_kernel(count, *refs):
    parts = refs[:count]
    weight = refs[count]
    outs = refs[count + 1 : count + 5]
    held = refs[count + 5]
    feat = weight.shape[0]
    heads = feat // HSZ
    stats = [part[feat:, :].astype(jnp.float32) for part in parts]
    for h in range(heads):
        rows = slice(h * HSZ, (h + 1) * HSZ)
        levels = [
            s[3 * h : 3 * h + 1] + s[3 * h + 1 : 3 * h + 2] + s[3 * h + 2 : 3 * h + 3] for s in stats
        ]
        peak = functools.reduce(jnp.maximum, levels)
        shares = [jnp.exp2(level - peak) for level in levels]
        total = functools.reduce(jnp.add, shares)
        summed = functools.reduce(
            jnp.add, [part[rows, :].astype(jnp.float32) * share for part, share in zip(parts, shares)]
        )
        held[:, rows] = (summed / total).T
    mine = lax.axis_index("mp")
    step = outs[0].shape[0]
    for k, out in enumerate(outs):
        start = pl.multiple_of(lax.rem(mine + k, 4) * step, step)
        attended = held[pl.ds(start, step), :].astype(jnp.bfloat16)
        out[...] = jnp.dot(attended, weight[...], preferred_element_type=jnp.float32).astype(
            out.dtype
        )


def project(parts, weight):
    feat, width = weight.shape
    rows = parts[0].shape[1]
    vmem = pl.BlockSpec(memory_space=pltpu.VMEM)
    return pl.pallas_call(
        functools.partial(project_kernel, len(parts)),
        out_shape=[jax.ShapeDtypeStruct((rows // 4, width), jnp.bfloat16)] * 4,
        in_specs=[vmem] * (len(parts) + 1),
        out_specs=[vmem] * 4,
        scratch_shapes=[pltpu.VMEM((rows, feat), jnp.float32)],
        compiler_params=pltpu.CompilerParams(vmem_limit_bytes=40 * 2**20),
        cost_estimate=pl.CostEstimate(
            flops=2 * rows * feat * width, bytes_accessed=2 * feat * width, transcendentals=0
        ),
        name="project",
    )(*parts, weight)


def head_kernel(
    group_branch, guidance_w, frame_level, p0, p1, p2, p3, residual, table, weight, out, held, sem
):
    rows, width = residual.shape
    token = (lax.axis_index("seq") * 4 + lax.axis_index("mp")) * rows
    level = frame_level[token // FRAME_TOK]
    fetch = pltpu.make_async_copy(table.at[level], held, sem)
    fetch.start()
    stream = residual[...].astype(jnp.float32) + (
        (p0[...].astype(jnp.float32) + p1[...].astype(jnp.float32))
        + (p2[...].astype(jnp.float32) + p3[...].astype(jnp.float32))
    )
    mean = jnp.mean(stream, axis=1, keepdims=True)
    centred = stream - mean
    variance = jnp.mean(centred * centred, axis=1, keepdims=True)
    normed = centred * lax.rsqrt(variance + 1e-06)
    fetch.wait()
    modulated = (normed * (1.0 + held[1:2, :]) + held[0:1, :]).astype(jnp.bfloat16)
    velocity = jnp.dot(modulated, weight[...], preferred_element_type=jnp.float32)
    out[...] = velocity * guidance_w[group_branch[lax.axis_index("branch")]]


def head(group_branch, guidance_w, frame_level, parts, residual, table, weight):
    rows, width = residual.shape
    vmem = pl.BlockSpec(memory_space=pltpu.VMEM)
    smem = pl.BlockSpec(memory_space=pltpu.SMEM)
    return pl.pallas_call(
        head_kernel,
        out_shape=jax.ShapeDtypeStruct((rows, weight.shape[1]), jnp.float32),
        in_specs=[smem] * 3 + [vmem] * 5 + [pl.BlockSpec(memory_space=pl.ANY), vmem],
        out_specs=vmem,
        scratch_shapes=[pltpu.VMEM(table.shape[1:], jnp.float32), pltpu.SemaphoreType.DMA],
        compiler_params=pltpu.CompilerParams(vmem_limit_bytes=40 * 2**20),
        name="head",
    )(group_branch, guidance_w, frame_level, *parts, residual, table, weight)


def body(
    span_q,
    span_k,
    span_v,
    hist_k,
    hist_v,
    hist_len,
    group_branch,
    guidance_w,
    frame_level,
    residual,
    out_weight,
    mod_table,
    head_weight,
):
    q = span_q[0]
    moves = [(0, 0), (1, 0), (0, 1), (0, 3), (1, 1), (1, 3), (0, 2), (1, 2)]
    queries = [q if m == (0, 0) else lax.ppermute(q, "seq", hop(*m, 0)) for m in moves]
    mine = [span_k[0], span_v[0], hist_k[0], hist_v[0]]
    theirs = [lax.ppermute(a, "seq", hop(0, 0, 1)) for a in mine]
    keys = [mine[0], theirs[0], mine[2], theirs[2]]
    values = [mine[1], theirs[1], mine[3], theirs[3]]
    partial = attend(hist_len, group_branch, queries[:4], keys, values, 4)
    partial += attend(hist_len, group_branch, queries[4:], keys, values, 4)
    parts = [
        p if m == (0, 0) else lax.ppermute(p, "seq", hop(m[0], -m[1], 0))
        for m, p in zip(moves, partial)
    ]
    blocks = project(parts, out_weight)
    reduced = [blocks[0]] + [lax.ppermute(blocks[k], "mp", turn(k)) for k in (1, 3, 2)]
    velocity = head(
        group_branch, guidance_w, frame_level, reduced, residual[0], mod_table, head_weight
    )
    around = [lax.ppermute(velocity, "branch", turn(k)) for k in (1, 3, 2)]
    return (velocity + around[2]) + (around[0] + around[1])


def solution(mesh):
    in_specs = (
        P("branch", "seq", "mp"),
        P("branch", "seq", "mp"),
        P("branch", "seq", "mp"),
        P("branch", "seq", "mp"),
        P("branch", "seq", "mp"),
        P(),
        P(),
        P(),
        P(),
        P("branch", ("seq", "mp"), None),
        P("mp", None),
        P(),
        P(),
    )
    out_specs = P(("seq", "mp"), None)
    return jax.shard_map(body, mesh=mesh, in_specs=in_specs, out_specs=out_specs, check_vma=False)
```

```python
import functools

import jax
import jax.numpy as jnp
from jax import lax
from jax.experimental import pallas as pl
from jax.experimental.pallas import tpu as pltpu
from jax.sharding import PartitionSpec as P

HSZ = 128
FRAME_TOK = 64
NEG = -1e30
LANES = 128
STAT_ROWS = 16
SCORE_TO_EXP2 = HSZ ** (-0.5) * 1.4426950408889634

XS = 4
MPS = 4


def hop(dz, dx, dc):
    return [
        ((z * XS + x) * 2 + c, ((z ^ dz) * XS + (x + dx) % XS) * 2 + (c ^ dc))
        for z in range(2)
        for x in range(XS)
        for c in range(2)
    ]


def pair_hop(place):
    pairs = []
    for z in range(2):
        for m in range(MPS):
            to_z, to_m = place(z, m)
            for r in range(XS * 2):
                pairs.append(
                    ((z * XS * 2 + r) * MPS + m, (to_z * XS * 2 + r) * MPS + to_m % MPS)
                )
    return pairs


def onward(z, m):
    return z, m + 2 * z - 1


def across_onward(z, m):
    return 1 - z, m + 2 * z - 1


def turn(step, count=4):
    return [(i, (i + step) % count) for i in range(count)]


def join_kernel(here, there, out):
    step = here.shape[0] // MPS
    mine = lax.axis_index("mp")
    side = lax.axis_index("seq") // (XS * 2)
    at = 0
    for first, second, toward in ((there, here, 3 - 2 * side), (here, there, 1 + 2 * side)):
        for ref, k in ((first, toward), (first, 2), (second, toward), (second, 0)):
            start = pl.multiple_of(lax.rem(mine + k, MPS) * step, step)
            out[at : at + step, :] = ref[pl.ds(start, step), :]
            at += step


def join(here, there):
    rows, feat = here.shape
    vmem = pl.BlockSpec(memory_space=pltpu.VMEM)
    return pl.pallas_call(
        join_kernel,
        out_shape=jax.ShapeDtypeStruct((2 * rows, feat), here.dtype),
        in_specs=[vmem] * 2,
        out_specs=vmem,
        compiler_params=pltpu.CompilerParams(vmem_limit_bytes=4 * 2**20),
        name="join",
    )(here, there)


def pack_kernel(
    span_q,
    span_k,
    span_v,
    hist_k,
    hist_v,
    hist_len,
    group_branch,
    out,
    bias,
    held,
    near_v,
    far_v,
    lens,
    order,
    sems,
):
    near, feat = span_k.shape
    far = hist_k.shape[0]
    count = near + far
    fetches = [
        pltpu.make_async_copy(source, target, sems.at[i])
        for i, (source, target) in enumerate(
            (
                (span_v, near_v),
                (hist_v, far_v),
                (span_k, out.at[:near]),
                (hist_k, out.at[near:count]),
                (hist_len, lens),
                (group_branch, order),
                (span_q, held),
            )
        )
    ]
    for fetch in fetches:
        fetch.start()
    fetches[0].wait()
    out[count:, :near] = near_v[...].T
    fetches[1].wait()
    out[count:, near:] = far_v[...].T
    for fetch in fetches[2:]:
        fetch.wait()
    length = lens[order[lax.axis_index("branch")]]
    seq = lax.axis_index("seq")
    lanes = bias.shape[1]
    for i, place in enumerate((seq, seq + 1 - 2 * lax.rem(seq, 2))):
        spot = place * far + lax.broadcasted_iota(jnp.int32, (far, lanes), 0)
        bias[i * count : i * count + near, :] = jnp.zeros((near, lanes), jnp.float32)
        bias[i * count + near : (i + 1) * count, :] = jnp.where(spot < length, 0.0, NEG)


def pack(span_q, span_k, span_v, hist_k, hist_v, hist_len, group_branch):
    near, feat = span_k.shape
    far = hist_k.shape[0]
    count = near + far
    vmem = pl.BlockSpec(memory_space=pltpu.VMEM)
    return pl.pallas_call(
        pack_kernel,
        out_shape=[
            jax.ShapeDtypeStruct((count + feat, feat), span_k.dtype),
            jax.ShapeDtypeStruct((2 * count, LANES), jnp.float32),
            jax.ShapeDtypeStruct(span_q.shape, span_q.dtype),
        ],
        in_specs=[pl.BlockSpec(memory_space=pltpu.HBM)] * 7,
        out_specs=[vmem] * 3,
        scratch_shapes=[
            pltpu.VMEM((near, feat), span_v.dtype),
            pltpu.VMEM((far, feat), hist_v.dtype),
            pltpu.SMEM(hist_len.shape, jnp.int32),
            pltpu.SMEM(group_branch.shape, jnp.int32),
            pltpu.SemaphoreType.DMA((7,)),
        ],
        compiler_params=pltpu.CompilerParams(vmem_limit_bytes=8 * 2**20),
        cost_estimate=pl.CostEstimate(flops=6 * 10**9, bytes_accessed=4 * count * feat, transcendentals=0),
        name="pack",
    )(
        *[
            pltpu.with_memory_space_constraint(a, pltpu.HBM)
            for a in (span_q, span_k, span_v, hist_k, hist_v, hist_len, group_branch)
        ]
    )


def attend_kernel(queries, mine_pack, core_pack, bias, *rest):
    sent = rest[-1]
    packs = (mine_pack, core_pack)
    feat = queries.shape[1]
    rows = queries.shape[0] // 2
    heads = feat // HSZ
    count = mine_pack.shape[0] - feat
    levels = []
    for h in range(heads):
        cols = slice(h * HSZ, (h + 1) * HSZ)
        q = queries[:, cols]
        scores = []
        for i, pack_ref in enumerate(packs):
            s = lax.dot_general(
                pack_ref[:count, cols],
                q,
                (((1,), (1,)), ((), ())),
                preferred_element_type=jnp.float32,
            )
            offset = bias[i * count : (i + 1) * count, :]
            scores.append(s + jnp.concatenate([offset] * (s.shape[1] // LANES), axis=1))
        peak = functools.reduce(jnp.maximum, [jnp.max(s, axis=0, keepdims=True) for s in scores])
        total, summed = 0.0, 0.0
        for pack_ref, s in zip(packs, scores):
            weights = jnp.exp2((s - peak) * SCORE_TO_EXP2)
            total = total + jnp.sum(weights, axis=0, keepdims=True)
            summed = summed + jnp.dot(
                pack_ref[count + h * HSZ : count + (h + 1) * HSZ, :],
                weights.astype(jnp.bfloat16),
                preferred_element_type=jnp.float32,
            )
        out = (summed / total).astype(jnp.bfloat16)
        for i in range(2):
            start = i * (feat + STAT_ROWS) + h * HSZ
            sent[start : start + HSZ, :] = out[:, i * rows : (i + 1) * rows]
        levels.append(peak * SCORE_TO_EXP2 + jnp.log2(total))
    stats = stat_rows(levels)
    for i in range(2):
        start = i * (feat + STAT_ROWS) + feat
        sent[start : start + STAT_ROWS, :] = stats[:, i * rows : (i + 1) * rows]


def stat_rows(levels):
    level = jnp.concatenate(levels, axis=0)
    high = level.astype(jnp.bfloat16).astype(jnp.float32)
    middle = (level - high).astype(jnp.bfloat16).astype(jnp.float32)
    spare = jnp.zeros((STAT_ROWS - 3 * level.shape[0], level.shape[1]), jnp.float32)
    return jnp.concatenate([high, middle, level - high - middle, spare], axis=0).astype(jnp.bfloat16)


def attend(queries, packs, bias, after):
    rows, feat = queries.shape[0] // 2, queries.shape[1]
    count = packs[0].shape[0] - feat
    vmem = pl.BlockSpec(memory_space=pltpu.VMEM)
    return pl.pallas_call(
        attend_kernel,
        out_shape=jax.ShapeDtypeStruct((2 * (feat + STAT_ROWS), rows), jnp.bfloat16),
        in_specs=[vmem] * 4 + [pl.BlockSpec(memory_space=pl.ANY)] * len(after),
        out_specs=vmem,
        compiler_params=pltpu.CompilerParams(vmem_limit_bytes=16 * 2**20),
        cost_estimate=pl.CostEstimate(
            flops=16 * rows * count * feat,
            bytes_accessed=8 * count * feat,
            transcendentals=4 * rows * count * (feat // HSZ),
        ),
        name="attend",
    )(queries, *packs, bias, *after)


def merged(parts, heads):
    feat = heads * HSZ
    levels = []
    for ref, at in parts:
        s = ref[at + feat : at + feat + STAT_ROWS, :].astype(jnp.float32)
        levels.append(s[:heads] + s[heads : 2 * heads] + s[2 * heads : 3 * heads])
    peak = functools.reduce(jnp.maximum, levels)
    shares = [jnp.exp2(level - peak) for level in levels]
    total = functools.reduce(jnp.add, shares)
    over = 1.0 / total
    shares = [share * over for share in shares]
    sums = [
        functools.reduce(
            jnp.add,
            [
                ref[at + h * HSZ : at + (h + 1) * HSZ, :].astype(jnp.float32) * share[h : h + 1]
                for (ref, at), share in zip(parts, shares)
            ],
        )
        for h in range(heads)
    ]
    return sums, peak + jnp.log2(total)


def merge_kernel(*refs):
    out = refs[-1]
    feat = out.shape[0] - STAT_ROWS
    sums, level = merged([(ref, out.shape[0]) for ref in refs[:-1]], feat // HSZ)
    for h, summed in enumerate(sums):
        out[h * HSZ : (h + 1) * HSZ, :] = summed.astype(jnp.bfloat16)
    out[feat:, :] = stat_rows([level])


def merge(parts):
    height, rows = parts[0].shape
    vmem = pl.BlockSpec(memory_space=pltpu.VMEM)
    return pl.pallas_call(
        merge_kernel,
        out_shape=jax.ShapeDtypeStruct((height // 2, rows), jnp.bfloat16),
        in_specs=[vmem] * len(parts),
        out_specs=vmem,
        compiler_params=pltpu.CompilerParams(vmem_limit_bytes=4 * 2**20),
        name="merge",
    )(*parts)


def project_kernel(count, *refs):
    parts = refs[:count]
    weight = refs[count]
    outs = refs[count + 1 : count + 1 + MPS]
    held = refs[count + 1 + MPS]
    feat, width = weight.shape
    for h, summed in enumerate(merged([(part, 0) for part in parts], feat // HSZ)[0]):
        held[:, h * HSZ : (h + 1) * HSZ] = summed.T.astype(jnp.bfloat16)
    step = outs[0].shape[0]
    chunk = 512
    for first in range(0, width, chunk):
        cols = slice(first, first + chunk)
        product = jnp.dot(held[...], weight[:, cols], preferred_element_type=jnp.float32)
        for i, out in enumerate(outs):
            out[:, cols] = product[i * step : (i + 1) * step].astype(out.dtype)


def project(parts, weight):
    feat, width = weight.shape
    rows = parts[0].shape[1]
    vmem = pl.BlockSpec(memory_space=pltpu.VMEM)
    return pl.pallas_call(
        functools.partial(project_kernel, len(parts)),
        out_shape=[jax.ShapeDtypeStruct((rows // MPS, width), jnp.bfloat16)] * MPS,
        in_specs=[vmem] * (len(parts) + 1),
        out_specs=[vmem] * MPS,
        scratch_shapes=[pltpu.VMEM((rows, feat), jnp.bfloat16)],
        compiler_params=pltpu.CompilerParams(vmem_limit_bytes=24 * 2**20),
        cost_estimate=pl.CostEstimate(
            flops=2 * rows * feat * width, bytes_accessed=2 * feat * width, transcendentals=0
        ),
        name="project",
    )(*parts, weight)


def head_kernel(
    group_branch, guidance_w, frame_level, p0, p1, p2, residual, table, weight, out, held, sem
):
    rows, width = residual.shape
    token = (lax.axis_index("seq") * 4 + lax.axis_index("mp")) * rows
    level = frame_level[token // FRAME_TOK]
    fetch = pltpu.make_async_copy(table.at[level], held, sem)
    fetch.start()
    stream = residual[...].astype(jnp.float32) + (
        (p0[...].astype(jnp.float32) + p1[...].astype(jnp.float32)) + p2[...].astype(jnp.float32)
    )
    mean = jnp.mean(stream, axis=1, keepdims=True)
    centred = stream - mean
    variance = jnp.mean(centred * centred, axis=1, keepdims=True)
    normed = centred * lax.rsqrt(variance + 1e-06)
    fetch.wait()
    modulated = (normed * (1.0 + held[1:2, :]) + held[0:1, :]).astype(jnp.bfloat16)
    velocity = jnp.dot(modulated, weight[...], preferred_element_type=jnp.float32)
    out[...] = velocity * guidance_w[group_branch[lax.axis_index("branch")]]


def head(group_branch, guidance_w, frame_level, parts, residual, table, weight):
    rows, width = residual.shape
    vmem = pl.BlockSpec(memory_space=pltpu.VMEM)
    smem = pl.BlockSpec(memory_space=pltpu.SMEM)
    return pl.pallas_call(
        head_kernel,
        out_shape=jax.ShapeDtypeStruct((rows, weight.shape[1]), jnp.float32),
        in_specs=[smem] * 3 + [vmem] * 4 + [pl.BlockSpec(memory_space=pl.ANY), vmem],
        out_specs=vmem,
        scratch_shapes=[pltpu.VMEM(table.shape[1:], jnp.float32), pltpu.SemaphoreType.DMA],
        compiler_params=pltpu.CompilerParams(vmem_limit_bytes=24 * 2**20),
        name="head",
    )(group_branch, guidance_w, frame_level, *parts, residual, table, weight)


def body(
    span_q,
    span_k,
    span_v,
    hist_k,
    hist_v,
    hist_len,
    group_branch,
    guidance_w,
    frame_level,
    residual,
    out_weight,
    mod_table,
    head_weight,
):
    mine = span_q[0]
    across = lax.ppermute(mine, "seq", hop(1, 0, 0))
    own, bias, held = pack(mine, span_k[0], span_v[0], hist_k[0], hist_v[0], hist_len, group_branch)
    packs = [own, lax.ppermute(own, "seq", hop(0, 0, 1))]
    pairs = {0: join(held, across)}
    for dx in (1, 3, 2):
        pairs[dx] = lax.ppermute(pairs[0], "seq", hop(0, dx, 0))
    parts = []
    made = []
    for dx in (0, 1, 3, 2):
        sent = attend(pairs[dx], packs, bias, made[-1:])
        made.append(sent)
        parts.append(lax.ppermute(sent, "seq", hop(0, -dx, 0)) if dx else sent)
    parts.append(lax.ppermute(merge(parts), "seq", hop(1, 0, 0)))
    near_block, far_block, side_block, own_block = project(parts, out_weight)
    passed = lax.ppermute(far_block, ("seq", "mp"), pair_hop(onward))
    aside = lax.ppermute(side_block, ("seq", "mp"), pair_hop(onward))
    joined = (near_block.astype(jnp.float32) + passed.astype(jnp.float32)).astype(jnp.bfloat16)
    reduced = [own_block, aside, lax.ppermute(joined, ("seq", "mp"), pair_hop(across_onward))]
    velocity = head(
        group_branch, guidance_w, frame_level, reduced, residual[0], mod_table, head_weight
    )
    around = [lax.ppermute(velocity, "branch", turn(k)) for k in (1, 3, 2)]
    return (velocity + around[2]) + (around[0] + around[1])


def solution(mesh):
    in_specs = (
        P("branch", "seq", "mp"),
        P("branch", "seq", "mp"),
        P("branch", "seq", "mp"),
        P("branch", "seq", "mp"),
        P("branch", "seq", "mp"),
        P(),
        P(),
        P(),
        P(),
        P("branch", ("seq", "mp"), None),
        P("mp", None),
        P(),
        P(),
    )
    out_specs = P(("seq", "mp"), None)
    return jax.shard_map(body, mesh=mesh, in_specs=in_specs, out_specs=out_specs, check_vma=False)
```

```python
import functools

import jax
import jax.numpy as jnp
from jax import lax
from jax.experimental import pallas as pl
from jax.experimental.pallas import tpu as pltpu
from jax.sharding import PartitionSpec as P

HSZ = 128
FRAME_TOK = 64
NEG = -1e30
LANES = 128
STAT_ROWS = 16
SCORE_TO_EXP2 = HSZ ** (-0.5) * 1.4426950408889634

XS = 4
MPS = 4


def hop(dz, dx, dc):
    return [
        ((z * XS + x) * 2 + c, ((z ^ dz) * XS + (x + dx) % XS) * 2 + (c ^ dc))
        for z in range(2)
        for x in range(XS)
        for c in range(2)
    ]


def pair_hop(place):
    pairs = []
    for z in range(2):
        for m in range(MPS):
            to_z, to_m = place(z, m)
            for r in range(XS * 2):
                pairs.append(
                    ((z * XS * 2 + r) * MPS + m, (to_z * XS * 2 + r) * MPS + to_m % MPS)
                )
    return pairs


def onward(z, m):
    return z, m + 2 * z - 1


def across_onward(z, m):
    return 1 - z, m + 2 * z - 1


def turn(step, count=4):
    return [(i, (i + step) % count) for i in range(count)]


def hold_kernel(source, *rest):
    rest[-1][...] = source[...]


def hold(source, after):
    vmem = pl.BlockSpec(memory_space=pltpu.VMEM)
    return pl.pallas_call(
        hold_kernel,
        out_shape=jax.ShapeDtypeStruct(source.shape, source.dtype),
        in_specs=[vmem] + [pl.BlockSpec(memory_space=pl.ANY)] * len(after),
        out_specs=vmem,
        compiler_params=pltpu.CompilerParams(vmem_limit_bytes=4 * 2**20),
        name="hold",
    )(source, *after)


def pack_kernel(
    span_q,
    span_k,
    span_v,
    hist_k,
    hist_v,
    hist_len,
    group_branch,
    out,
    bias,
    queries,
    near_v,
    far_v,
    held,
    lens,
    order,
    sems,
):
    near, feat = span_k.shape
    far = hist_k.shape[0]
    count = near + far
    fetches = [
        pltpu.make_async_copy(source, target, sems.at[i])
        for i, (source, target) in enumerate(
            (
                (span_v, near_v),
                (hist_v, far_v),
                (span_k, out.at[:near]),
                (hist_k, out.at[near:count]),
                (hist_len, lens),
                (group_branch, order),
                (span_q, held),
            )
        )
    ]
    for fetch in fetches:
        fetch.start()
    fetches[0].wait()
    out[count:, :near] = near_v[...].T
    fetches[1].wait()
    out[count:, near:] = far_v[...].T
    for fetch in fetches[2:]:
        fetch.wait()
    step = held.shape[0] // MPS
    mine = lax.axis_index("mp")
    side = lax.axis_index("seq") // (XS * 2)
    for i, k in enumerate((3 - 2 * side, 0, 1 + 2 * side, 2)):
        start = pl.multiple_of(lax.rem(mine + k, MPS) * step, step)
        queries[i * step : (i + 1) * step, :] = held[pl.ds(start, step), :]
    length = lens[order[lax.axis_index("branch")]]
    seq = lax.axis_index("seq")
    lanes = bias.shape[1]
    for i, place in enumerate((seq, seq + 1 - 2 * lax.rem(seq, 2))):
        spot = place * far + lax.broadcasted_iota(jnp.int32, (far, lanes), 0)
        bias[i * count : i * count + near, :] = jnp.zeros((near, lanes), jnp.float32)
        bias[i * count + near : (i + 1) * count, :] = jnp.where(spot < length, 0.0, NEG)


def pack(span_q, span_k, span_v, hist_k, hist_v, hist_len, group_branch):
    near, feat = span_k.shape
    far = hist_k.shape[0]
    count = near + far
    vmem = pl.BlockSpec(memory_space=pltpu.VMEM)
    return pl.pallas_call(
        pack_kernel,
        out_shape=[
            jax.ShapeDtypeStruct((count + feat, feat), span_k.dtype),
            jax.ShapeDtypeStruct((2 * count, LANES), jnp.float32),
            jax.ShapeDtypeStruct(span_q.shape, span_q.dtype),
        ],
        in_specs=[pl.BlockSpec(memory_space=pltpu.HBM)] * 7,
        out_specs=[vmem] * 3,
        scratch_shapes=[
            pltpu.VMEM((near, feat), span_v.dtype),
            pltpu.VMEM((far, feat), hist_v.dtype),
            pltpu.VMEM(span_q.shape, span_q.dtype),
            pltpu.SMEM(hist_len.shape, jnp.int32),
            pltpu.SMEM(group_branch.shape, jnp.int32),
            pltpu.SemaphoreType.DMA((7,)),
        ],
        compiler_params=pltpu.CompilerParams(vmem_limit_bytes=8 * 2**20),
        cost_estimate=pl.CostEstimate(flops=6 * 10**9, bytes_accessed=4 * count * feat, transcendentals=0),
        name="pack",
    )(
        *[
            pltpu.with_memory_space_constraint(a, pltpu.HBM)
            for a in (span_q, span_k, span_v, hist_k, hist_v, hist_len, group_branch)
        ]
    )


def attend_kernel(here, there, mine_pack, core_pack, bias, *rest):
    sent = rest[-1]
    packs = (mine_pack, core_pack)
    rows, feat = here.shape
    half = rows // 2
    heads = feat // HSZ
    count = mine_pack.shape[0] - feat
    levels = []

    def scores_of(h):
        cols = slice(h * HSZ, (h + 1) * HSZ)
        q = jnp.concatenate(
            [there[half:, cols], here[:half, cols], here[half:, cols], there[:half, cols]], axis=0
        )
        scores = []
        for i, pack_ref in enumerate(packs):
            s = lax.dot_general(
                pack_ref[:count, cols],
                q,
                (((1,), (1,)), ((), ())),
                preferred_element_type=jnp.float32,
            )
            offset = bias[i * count : (i + 1) * count, :]
            scores.append(s + jnp.concatenate([offset] * (s.shape[1] // LANES), axis=1))
        return scores

    coming = scores_of(0)
    for h in range(heads):
        scores = coming
        if h + 1 < heads:
            coming = scores_of(h + 1)
        peak = functools.reduce(jnp.maximum, [jnp.max(s, axis=0, keepdims=True) for s in scores])
        total, summed = 0.0, 0.0
        for pack_ref, s in zip(packs, scores):
            weights = jnp.exp2((s - peak) * SCORE_TO_EXP2)
            total = total + jnp.sum(weights, axis=0, keepdims=True)
            summed = summed + jnp.dot(
                pack_ref[count + h * HSZ : count + (h + 1) * HSZ, :],
                weights.astype(jnp.bfloat16),
                preferred_element_type=jnp.float32,
            )
        out = (summed / total).astype(jnp.bfloat16)
        for i in range(2):
            start = i * (feat + STAT_ROWS) + h * HSZ
            sent[start : start + HSZ, :] = out[:, i * rows : (i + 1) * rows]
        levels.append(peak * SCORE_TO_EXP2 + jnp.log2(total))
    stats = stat_rows(levels)
    for i in range(2):
        start = i * (feat + STAT_ROWS) + feat
        sent[start : start + STAT_ROWS, :] = stats[:, i * rows : (i + 1) * rows]


def stat_rows(levels):
    level = jnp.concatenate(levels, axis=0)
    high = level.astype(jnp.bfloat16).astype(jnp.float32)
    middle = (level - high).astype(jnp.bfloat16).astype(jnp.float32)
    spare = jnp.zeros((STAT_ROWS - 3 * level.shape[0], level.shape[1]), jnp.float32)
    return jnp.concatenate([high, middle, level - high - middle, spare], axis=0).astype(jnp.bfloat16)


def attend(queries, packs, bias, after):
    rows, feat = queries[0].shape
    count = packs[0].shape[0] - feat
    vmem = pl.BlockSpec(memory_space=pltpu.VMEM)
    return pl.pallas_call(
        attend_kernel,
        out_shape=jax.ShapeDtypeStruct((2 * (feat + STAT_ROWS), rows), jnp.bfloat16),
        in_specs=[vmem] * 5 + [pl.BlockSpec(memory_space=pl.ANY)] * len(after),
        out_specs=vmem,
        compiler_params=pltpu.CompilerParams(vmem_limit_bytes=16 * 2**20),
        cost_estimate=pl.CostEstimate(
            flops=16 * rows * count * feat,
            bytes_accessed=8 * count * feat,
            transcendentals=4 * rows * count * (feat // HSZ),
        ),
        name="attend",
    )(*queries, *packs, bias, *after)


def merged(parts, heads):
    feat = heads * HSZ
    levels = []
    for ref, at in parts:
        s = ref[at + feat : at + feat + STAT_ROWS, :].astype(jnp.float32)
        levels.append(s[:heads] + s[heads : 2 * heads] + s[2 * heads : 3 * heads])
    peak = functools.reduce(jnp.maximum, levels)
    shares = [jnp.exp2(level - peak) for level in levels]
    total = functools.reduce(jnp.add, shares)
    over = 1.0 / total
    shares = [share * over for share in shares]
    sums = [
        functools.reduce(
            jnp.add,
            [
                ref[at + h * HSZ : at + (h + 1) * HSZ, :].astype(jnp.float32) * share[h : h + 1]
                for (ref, at), share in zip(parts, shares)
            ],
        )
        for h in range(heads)
    ]
    return sums, peak + jnp.log2(total)


def merge_kernel(*refs):
    out = refs[-1]
    feat = out.shape[0] - STAT_ROWS
    sums, level = merged([(ref, out.shape[0]) for ref in refs[:-1]], feat // HSZ)
    for h, summed in enumerate(sums):
        out[h * HSZ : (h + 1) * HSZ, :] = summed.astype(jnp.bfloat16)
    out[feat:, :] = stat_rows([level])


def merge(parts):
    height, rows = parts[0].shape
    vmem = pl.BlockSpec(memory_space=pltpu.VMEM)
    return pl.pallas_call(
        merge_kernel,
        out_shape=jax.ShapeDtypeStruct((height // 2, rows), jnp.bfloat16),
        in_specs=[vmem] * len(parts),
        out_specs=vmem,
        compiler_params=pltpu.CompilerParams(vmem_limit_bytes=4 * 2**20),
        name="merge",
    )(*parts)


def project_kernel(count, *refs):
    parts = refs[:count]
    weight = refs[count]
    outs = refs[count + 1 : count + 1 + MPS]
    held = refs[count + 1 + MPS]
    feat, width = weight.shape
    for h, summed in enumerate(merged([(part, 0) for part in parts], feat // HSZ)[0]):
        held[:, h * HSZ : (h + 1) * HSZ] = summed.T.astype(jnp.bfloat16)
    step = outs[0].shape[0]
    chunk = 512
    for first in range(0, width, chunk):
        cols = slice(first, first + chunk)
        product = jnp.dot(held[...], weight[:, cols], preferred_element_type=jnp.float32)
        for i, out in enumerate(outs):
            out[:, cols] = product[i * step : (i + 1) * step].astype(out.dtype)


def project(parts, weight):
    feat, width = weight.shape
    rows = parts[0].shape[1]
    vmem = pl.BlockSpec(memory_space=pltpu.VMEM)
    return pl.pallas_call(
        functools.partial(project_kernel, len(parts)),
        out_shape=[jax.ShapeDtypeStruct((rows // MPS, width), jnp.bfloat16)] * MPS,
        in_specs=[vmem] * (len(parts) + 1),
        out_specs=[vmem] * MPS,
        scratch_shapes=[pltpu.VMEM((rows, feat), jnp.bfloat16)],
        compiler_params=pltpu.CompilerParams(vmem_limit_bytes=24 * 2**20),
        cost_estimate=pl.CostEstimate(
            flops=2 * rows * feat * width, bytes_accessed=2 * feat * width, transcendentals=0
        ),
        name="project",
    )(*parts, weight)


def head_kernel(
    group_branch, guidance_w, frame_level, p0, p1, p2, residual, table, weight, out, held, sem
):
    rows, width = residual.shape
    token = (lax.axis_index("seq") * 4 + lax.axis_index("mp")) * rows
    level = frame_level[token // FRAME_TOK]
    fetch = pltpu.make_async_copy(table.at[level], held, sem)
    fetch.start()
    stream = residual[...].astype(jnp.float32) + (
        (p0[...].astype(jnp.float32) + p1[...].astype(jnp.float32)) + p2[...].astype(jnp.float32)
    )
    mean = jnp.mean(stream, axis=1, keepdims=True)
    centred = stream - mean
    variance = jnp.mean(centred * centred, axis=1, keepdims=True)
    normed = centred * lax.rsqrt(variance + 1e-06)
    fetch.wait()
    modulated = (normed * (1.0 + held[1:2, :]) + held[0:1, :]).astype(jnp.bfloat16)
    velocity = jnp.dot(modulated, weight[...], preferred_element_type=jnp.float32)
    out[...] = velocity * guidance_w[group_branch[lax.axis_index("branch")]]


def head(group_branch, guidance_w, frame_level, parts, residual, table, weight):
    rows, width = residual.shape
    vmem = pl.BlockSpec(memory_space=pltpu.VMEM)
    smem = pl.BlockSpec(memory_space=pltpu.SMEM)
    return pl.pallas_call(
        head_kernel,
        out_shape=jax.ShapeDtypeStruct((rows, weight.shape[1]), jnp.float32),
        in_specs=[smem] * 3 + [vmem] * 4 + [pl.BlockSpec(memory_space=pl.ANY), vmem],
        out_specs=vmem,
        scratch_shapes=[pltpu.VMEM(table.shape[1:], jnp.float32), pltpu.SemaphoreType.DMA],
        compiler_params=pltpu.CompilerParams(vmem_limit_bytes=24 * 2**20),
        name="head",
    )(group_branch, guidance_w, frame_level, *parts, residual, table, weight)


def body(
    span_q,
    span_k,
    span_v,
    hist_k,
    hist_v,
    hist_len,
    group_branch,
    guidance_w,
    frame_level,
    residual,
    out_weight,
    mod_table,
    head_weight,
):
    own, bias, mine = pack(
        span_q[0], span_k[0], span_v[0], hist_k[0], hist_v[0], hist_len, group_branch
    )
    packs = [own, lax.ppermute(own, "seq", hop(0, 0, 1))]
    across = lax.ppermute(mine, "seq", hop(1, 0, 0))
    up, down = hop(0, 1, 0), hop(0, 3, 0)
    mine_up, mine_down = lax.ppermute(mine, "seq", up), lax.ppermute(mine, "seq", down)
    ready = hold(across, [mine_up, mine_down])
    across_up, across_down = lax.ppermute(ready, "seq", up), lax.ppermute(ready, "seq", down)
    pairs = {
        0: (mine, across),
        1: (mine_up, across_up),
        3: (mine_down, across_down),
        2: (lax.ppermute(mine_up, "seq", up), lax.ppermute(across_down, "seq", down)),
    }
    parts = []
    made = []
    for dx in (0, 1, 3, 2):
        sent = attend(pairs[dx], packs, bias, ())
        made.append(sent)
        parts.append(lax.ppermute(sent, "seq", hop(0, -dx, 0)) if dx else sent)
    parts.append(lax.ppermute(merge(parts), "seq", hop(1, 0, 0)))
    near_block, far_block, side_block, own_block = project(parts, out_weight)
    passed = lax.ppermute(far_block, ("seq", "mp"), pair_hop(onward))
    aside = lax.ppermute(side_block, ("seq", "mp"), pair_hop(onward))
    joined = (near_block.astype(jnp.float32) + passed.astype(jnp.float32)).astype(jnp.bfloat16)
    reduced = [own_block, aside, lax.ppermute(joined, ("seq", "mp"), pair_hop(across_onward))]
    velocity = head(
        group_branch, guidance_w, frame_level, reduced, residual[0], mod_table, head_weight
    )
    around = [lax.ppermute(velocity, "branch", turn(k)) for k in (1, 3, 2)]
    return (velocity + around[2]) + (around[0] + around[1])


def solution(mesh):
    in_specs = (
        P("branch", "seq", "mp"),
        P("branch", "seq", "mp"),
        P("branch", "seq", "mp"),
        P("branch", "seq", "mp"),
        P("branch", "seq", "mp"),
        P(),
        P(),
        P(),
        P(),
        P("branch", ("seq", "mp"), None),
        P("mp", None),
        P(),
        P(),
    )
    out_specs = P(("seq", "mp"), None)
    return jax.shard_map(body, mesh=mesh, in_specs=in_specs, out_specs=out_specs, check_vma=False)
```

```python
import functools

import jax
import jax.numpy as jnp
from jax import lax
from jax.experimental import pallas as pl
from jax.experimental.pallas import tpu as pltpu
from jax.sharding import PartitionSpec as P

HSZ = 128
FRAME_TOK = 64
NEG = -1e30
LANES = 128
STAT_ROWS = 16
SCORE_TO_EXP2 = HSZ ** (-0.5) * 1.4426950408889634

XS = 4
MPS = 4


def hop(dz, dx, dc):
    return [
        ((z * XS + x) * 2 + c, ((z ^ dz) * XS + (x + dx) % XS) * 2 + (c ^ dc))
        for z in range(2)
        for x in range(XS)
        for c in range(2)
    ]


def pair_hop(place):
    pairs = []
    for z in range(2):
        for m in range(MPS):
            to_z, to_m = place(z, m)
            for r in range(XS * 2):
                pairs.append(
                    ((z * XS * 2 + r) * MPS + m, (to_z * XS * 2 + r) * MPS + to_m % MPS)
                )
    return pairs


def onward(z, m):
    return z, m + 2 * z - 1


def across_onward(z, m):
    return 1 - z, m + 2 * z - 1


def turn(step, count=4):
    return [(i, (i + step) % count) for i in range(count)]


def hold_kernel(source, *rest):
    rest[-1][...] = source[...]


def hold(source, after):
    vmem = pl.BlockSpec(memory_space=pltpu.VMEM)
    return pl.pallas_call(
        hold_kernel,
        out_shape=jax.ShapeDtypeStruct(source.shape, source.dtype),
        in_specs=[vmem] + [pl.BlockSpec(memory_space=pl.ANY)] * len(after),
        out_specs=vmem,
        compiler_params=pltpu.CompilerParams(vmem_limit_bytes=4 * 2**20),
        name="hold",
    )(source, *after)


def pack_kernel(
    span_q,
    span_k,
    span_v,
    hist_k,
    hist_v,
    hist_len,
    group_branch,
    out,
    bias,
    queries,
    near_v,
    far_v,
    held,
    lens,
    order,
    sems,
):
    near, feat = span_k.shape
    far = hist_k.shape[0]
    count = near + far
    fetches = [
        pltpu.make_async_copy(source, target, sems.at[i])
        for i, (source, target) in enumerate(
            (
                (span_v, near_v),
                (hist_v, far_v),
                (span_k, out.at[:near]),
                (hist_k, out.at[near:count]),
                (hist_len, lens),
                (group_branch, order),
                (span_q, held),
            )
        )
    ]
    for fetch in fetches:
        fetch.start()
    fetches[0].wait()
    out[count:, :near] = near_v[...].T
    fetches[1].wait()
    out[count:, near:] = far_v[...].T
    for fetch in fetches[2:]:
        fetch.wait()
    step = held.shape[0] // MPS
    mine = lax.axis_index("mp")
    side = lax.axis_index("seq") // (XS * 2)
    for i, k in enumerate((3 - 2 * side, 0, 1 + 2 * side, 2)):
        start = pl.multiple_of(lax.rem(mine + k, MPS) * step, step)
        queries[i * step : (i + 1) * step, :] = held[pl.ds(start, step), :]
    length = lens[order[lax.axis_index("branch")]]
    seq = lax.axis_index("seq")
    lanes = bias.shape[1]
    for i, place in enumerate((seq, seq + 1 - 2 * lax.rem(seq, 2))):
        spot = place * far + lax.broadcasted_iota(jnp.int32, (far, lanes), 0)
        bias[i * count : i * count + near, :] = jnp.zeros((near, lanes), jnp.float32)
        bias[i * count + near : (i + 1) * count, :] = jnp.where(spot < length, 0.0, NEG)


def pack(span_q, span_k, span_v, hist_k, hist_v, hist_len, group_branch):
    near, feat = span_k.shape
    far = hist_k.shape[0]
    count = near + far
    vmem = pl.BlockSpec(memory_space=pltpu.VMEM)
    return pl.pallas_call(
        pack_kernel,
        out_shape=[
            jax.ShapeDtypeStruct((count + feat, feat), span_k.dtype),
            jax.ShapeDtypeStruct((2 * count, LANES), jnp.float32),
            jax.ShapeDtypeStruct(span_q.shape, span_q.dtype),
        ],
        in_specs=[pl.BlockSpec(memory_space=pltpu.HBM)] * 7,
        out_specs=[vmem] * 3,
        scratch_shapes=[
            pltpu.VMEM((near, feat), span_v.dtype),
            pltpu.VMEM((far, feat), hist_v.dtype),
            pltpu.VMEM(span_q.shape, span_q.dtype),
            pltpu.SMEM(hist_len.shape, jnp.int32),
            pltpu.SMEM(group_branch.shape, jnp.int32),
            pltpu.SemaphoreType.DMA((7,)),
        ],
        compiler_params=pltpu.CompilerParams(vmem_limit_bytes=8 * 2**20),
        cost_estimate=pl.CostEstimate(flops=6 * 10**9, bytes_accessed=4 * count * feat, transcendentals=0),
        name="pack",
    )(
        *[
            pltpu.with_memory_space_constraint(a, pltpu.HBM)
            for a in (span_q, span_k, span_v, hist_k, hist_v, hist_len, group_branch)
        ]
    )


def attend_kernel(joins, first, second, mine_pack, core_pack, bias, *rest):
    packs = (mine_pack, core_pack)
    sent = rest[-2:]
    rows, feat = first.shape
    height = feat + STAT_ROWS
    heads = feat // HSZ
    count = mine_pack.shape[0] - feat
    levels = []

    def put(at, value):
        size = value.shape[0]
        for i in range(2):
            got = value[:, i * rows : (i + 1) * rows]
            if joins:
                partner = rest[i][at : at + size, :]
                low = lax.broadcasted_iota(jnp.int32, got.shape, 1) < rows // 2
                sent[i][at : at + size, :] = jnp.where(low, partner, got)
                sent[i][height + at : height + at + size, :] = jnp.where(low, got, partner)
            else:
                sent[i][at : at + size, :] = got

    def scores_of(h):
        cols = slice(h * HSZ, (h + 1) * HSZ)
        q = jnp.concatenate([first[:, cols], second[:, cols]], axis=0)
        scores = []
        for i, pack_ref in enumerate(packs):
            s = lax.dot_general(
                pack_ref[:count, cols],
                q,
                (((1,), (1,)), ((), ())),
                preferred_element_type=jnp.float32,
            )
            offset = bias[i * count : (i + 1) * count, :]
            scores.append(s + jnp.concatenate([offset] * (s.shape[1] // LANES), axis=1))
        return scores

    coming = scores_of(0)
    for h in range(heads):
        scores = coming
        if h + 1 < heads:
            coming = scores_of(h + 1)
        peak = functools.reduce(jnp.maximum, [jnp.max(s, axis=0, keepdims=True) for s in scores])
        total, summed = 0.0, 0.0
        for pack_ref, s in zip(packs, scores):
            weights = jnp.exp2((s - peak) * SCORE_TO_EXP2)
            total = total + jnp.sum(weights, axis=0, keepdims=True)
            summed = summed + jnp.dot(
                pack_ref[count + h * HSZ : count + (h + 1) * HSZ, :],
                weights.astype(jnp.bfloat16),
                preferred_element_type=jnp.float32,
            )
        put(h * HSZ, (summed / total).astype(jnp.bfloat16))
        levels.append(peak * SCORE_TO_EXP2 + jnp.log2(total))
    put(feat, stat_rows(levels))


def stat_rows(levels):
    level = jnp.concatenate(levels, axis=0)
    high = level.astype(jnp.bfloat16).astype(jnp.float32)
    middle = (level - high).astype(jnp.bfloat16).astype(jnp.float32)
    spare = jnp.zeros((STAT_ROWS - 3 * level.shape[0], level.shape[1]), jnp.float32)
    return jnp.concatenate([high, middle, level - high - middle, spare], axis=0).astype(jnp.bfloat16)


def attend(blocks, packs, bias, partners=(), after=()):
    rows, feat = blocks[0].shape
    count = packs[0].shape[0] - feat
    height = (feat + STAT_ROWS) * (2 if partners else 1)
    vmem = pl.BlockSpec(memory_space=pltpu.VMEM)
    return pl.pallas_call(
        functools.partial(attend_kernel, bool(partners)),
        out_shape=[jax.ShapeDtypeStruct((height, rows), jnp.bfloat16)] * 2,
        in_specs=[vmem] * (5 + len(partners)) + [pl.BlockSpec(memory_space=pl.ANY)] * len(after),
        out_specs=[vmem] * 2,
        compiler_params=pltpu.CompilerParams(vmem_limit_bytes=16 * 2**20),
        cost_estimate=pl.CostEstimate(
            flops=16 * rows * count * feat,
            bytes_accessed=8 * count * feat,
            transcendentals=4 * rows * count * (feat // HSZ),
        ),
        name="attend",
    )(*blocks, *packs, bias, *partners, *after)


def merged(parts, heads):
    feat = heads * HSZ
    levels = []
    for ref, at in parts:
        s = ref[at + feat : at + feat + STAT_ROWS, :].astype(jnp.float32)
        levels.append(s[:heads] + s[heads : 2 * heads] + s[2 * heads : 3 * heads])
    peak = functools.reduce(jnp.maximum, levels)
    shares = [jnp.exp2(level - peak) for level in levels]
    total = functools.reduce(jnp.add, shares)
    over = 1.0 / total
    shares = [share * over for share in shares]
    sums = [
        functools.reduce(
            jnp.add,
            [
                ref[at + h * HSZ : at + (h + 1) * HSZ, :].astype(jnp.float32) * share[h : h + 1]
                for (ref, at), share in zip(parts, shares)
            ],
        )
        for h in range(heads)
    ]
    return sums, peak + jnp.log2(total)


def merge_kernel(*refs):
    out = refs[-1]
    feat = out.shape[0] - STAT_ROWS
    sums, level = merged([(ref, out.shape[0]) for ref in refs[:-1]], feat // HSZ)
    for h, summed in enumerate(sums):
        out[h * HSZ : (h + 1) * HSZ, :] = summed.astype(jnp.bfloat16)
    out[feat:, :] = stat_rows([level])


def merge(parts):
    height, rows = parts[0].shape
    vmem = pl.BlockSpec(memory_space=pltpu.VMEM)
    return pl.pallas_call(
        merge_kernel,
        out_shape=jax.ShapeDtypeStruct((height // 2, rows), jnp.bfloat16),
        in_specs=[vmem] * len(parts),
        out_specs=vmem,
        compiler_params=pltpu.CompilerParams(vmem_limit_bytes=4 * 2**20),
        name="merge",
    )(*parts)


def project_kernel(count, *refs):
    parts = refs[:count]
    weight = refs[count]
    outs = refs[count + 1 : count + 1 + MPS]
    held = refs[count + 1 + MPS]
    feat, width = weight.shape
    for h, summed in enumerate(merged([(part, 0) for part in parts], feat // HSZ)[0]):
        held[:, h * HSZ : (h + 1) * HSZ] = summed.T.astype(jnp.bfloat16)
    step = outs[0].shape[0]
    chunk = 512
    for first in range(0, width, chunk):
        cols = slice(first, first + chunk)
        product = jnp.dot(held[...], weight[:, cols], preferred_element_type=jnp.float32)
        for i, out in enumerate(outs):
            out[:, cols] = product[i * step : (i + 1) * step].astype(out.dtype)


def project(parts, weight):
    feat, width = weight.shape
    rows = parts[0].shape[1]
    vmem = pl.BlockSpec(memory_space=pltpu.VMEM)
    return pl.pallas_call(
        functools.partial(project_kernel, len(parts)),
        out_shape=[jax.ShapeDtypeStruct((rows // MPS, width), jnp.bfloat16)] * MPS,
        in_specs=[vmem] * (len(parts) + 1),
        out_specs=[vmem] * MPS,
        scratch_shapes=[pltpu.VMEM((rows, feat), jnp.bfloat16)],
        compiler_params=pltpu.CompilerParams(vmem_limit_bytes=24 * 2**20),
        cost_estimate=pl.CostEstimate(
            flops=2 * rows * feat * width, bytes_accessed=2 * feat * width, transcendentals=0
        ),
        name="project",
    )(*parts, weight)


def add_kernel(first, second, out):
    out[...] = (first[...].astype(jnp.float32) + second[...].astype(jnp.float32)).astype(out.dtype)


def add(first, second):
    vmem = pl.BlockSpec(memory_space=pltpu.VMEM)
    return pl.pallas_call(
        add_kernel,
        out_shape=jax.ShapeDtypeStruct(first.shape, first.dtype),
        in_specs=[vmem] * 2,
        out_specs=vmem,
        compiler_params=pltpu.CompilerParams(vmem_limit_bytes=4 * 2**20),
        name="add",
    )(first, second)


def head_kernel(
    group_branch, guidance_w, frame_level, p0, p1, p2, residual, table, weight, out, held, sem
):
    rows, width = residual.shape
    token = (lax.axis_index("seq") * 4 + lax.axis_index("mp")) * rows
    level = frame_level[token // FRAME_TOK]
    fetch = pltpu.make_async_copy(table.at[level], held, sem)
    fetch.start()
    stream = residual[...].astype(jnp.float32) + (
        (p0[...].astype(jnp.float32) + p1[...].astype(jnp.float32)) + p2[...].astype(jnp.float32)
    )
    mean = jnp.mean(stream, axis=1, keepdims=True)
    centred = stream - mean
    variance = jnp.mean(centred * centred, axis=1, keepdims=True)
    normed = centred * lax.rsqrt(variance + 1e-06)
    fetch.wait()
    modulated = (normed * (1.0 + held[1:2, :]) + held[0:1, :]).astype(jnp.bfloat16)
    velocity = jnp.dot(modulated, weight[...], preferred_element_type=jnp.float32)
    out[...] = velocity * guidance_w[group_branch[lax.axis_index("branch")]]


def head(group_branch, guidance_w, frame_level, parts, residual, table, weight):
    rows, width = residual.shape
    vmem = pl.BlockSpec(memory_space=pltpu.VMEM)
    smem = pl.BlockSpec(memory_space=pltpu.SMEM)
    return pl.pallas_call(
        head_kernel,
        out_shape=jax.ShapeDtypeStruct((rows, weight.shape[1]), jnp.float32),
        in_specs=[smem] * 3 + [vmem] * 4 + [pl.BlockSpec(memory_space=pl.ANY), vmem],
        out_specs=vmem,
        scratch_shapes=[pltpu.VMEM(table.shape[1:], jnp.float32), pltpu.SemaphoreType.DMA],
        compiler_params=pltpu.CompilerParams(vmem_limit_bytes=24 * 2**20),
        name="head",
    )(group_branch, guidance_w, frame_level, *parts, residual, table, weight)


def body(
    span_q,
    span_k,
    span_v,
    hist_k,
    hist_v,
    hist_len,
    group_branch,
    guidance_w,
    frame_level,
    residual,
    out_weight,
    mod_table,
    head_weight,
):
    own, bias, mine = pack(
        span_q[0], span_k[0], span_v[0], hist_k[0], hist_v[0], hist_len, group_branch
    )
    packs = [own, lax.ppermute(own, "seq", hop(0, 0, 1))]
    across = lax.ppermute(mine, "seq", hop(1, 0, 0))
    up, down = hop(0, 1, 0), hop(0, 3, 0)
    mine_up, mine_down = lax.ppermute(mine, "seq", up), lax.ppermute(mine, "seq", down)
    ready = hold(across, [mine_up, mine_down])
    across_up, across_down = lax.ppermute(ready, "seq", up), lax.ppermute(ready, "seq", down)
    mine_two = lax.ppermute(mine_up, "seq", up)
    across_two = lax.ppermute(ready, "seq", hop(0, 2, 0))
    out_up, out_down = attend((mine_up, mine_down), packs, bias)
    out_two, out_own = attend((mine_two, mine), packs, bias)
    sent_up, sent_down = attend((across_up, across_down), packs, bias, (out_up, out_down))
    sent_two, sent_own = attend((across_two, across), packs, bias, (out_two, out_own))
    parts = [
        lax.ppermute(sent_up, "seq", down),
        lax.ppermute(sent_down, "seq", up),
        lax.ppermute(sent_two, "seq", hop(0, 2, 0)),
        sent_own,
    ]
    parts.append(lax.ppermute(merge(parts), "seq", hop(1, 0, 0)))
    side_block, own_block, near_block, far_block = project(parts, out_weight)
    passed = lax.ppermute(far_block, ("seq", "mp"), pair_hop(onward))
    aside = lax.ppermute(side_block, ("seq", "mp"), pair_hop(onward))
    joined = add(near_block, passed)
    reduced = [own_block, aside, lax.ppermute(joined, ("seq", "mp"), pair_hop(across_onward))]
    velocity = head(
        group_branch, guidance_w, frame_level, reduced, residual[0], mod_table, head_weight
    )
    around = [lax.ppermute(velocity, "branch", turn(k)) for k in (1, 3, 2)]
    return (velocity + around[2]) + (around[0] + around[1])


def solution(mesh):
    in_specs = (
        P("branch", "seq", "mp"),
        P("branch", "seq", "mp"),
        P("branch", "seq", "mp"),
        P("branch", "seq", "mp"),
        P("branch", "seq", "mp"),
        P(),
        P(),
        P(),
        P(),
        P("branch", ("seq", "mp"), None),
        P("mp", None),
        P(),
        P(),
    )
    out_specs = P(("seq", "mp"), None)
    return jax.shard_map(body, mesh=mesh, in_specs=in_specs, out_specs=out_specs, check_vma=False)
```
